32 devices in a mesh: grp: 4 (over z), tp: 4 (over y, x), seq: 2 (over core).
Axes of the slice: x: 2, y: 2, z: 4, core: 2. Of those that a mesh axis runs over, the one named last changes fastest.
Arguments:
- tokens: bfloat16 [4096, 4096], P(('grp', 'seq')), may hold values from -6 to 6
- base_weight: bfloat16 [4096, 1024], P(None, 'tp'), may hold values from -0.09375 to 0.09375
- adapter_a: bfloat16 [256, 16, 4096], P('grp', None, 'tp'), may hold values from -0.09375 to 0.09375
- adapter_b: bfloat16 [256, 16, 1024], P('grp', None, 'tp'), may hold values from -1.5 to 1.5
- token_tenant: int32 [4096], P(('grp', 'seq')), may hold values from 0 to 255, as said below
- tenant_lists: int32 [4, 4, 12], replicated, may hold values from -1 to 255, as said below
- cotangent: bfloat16 [4096, 1024], P(('grp', 'seq'), 'tp'), may hold values from -0.3125 to 0.3125
Outputs:
- projected: bfloat16 [4096, 1024], P(('grp', 'seq'), 'tp')
- grad_a: float32 [256, 16, 4096], P('grp', None, 'tp')
- grad_b: float32 [256, 16, 1024], P('grp', None, 'tp')
The draws below stay inside these ranges and needn't reach their ends.
Inputs may be any that keep to these rules, and one draw needn't show every extreme that they name: `token_tenant`: every token's tenant is a live entry of its data group's list. `tenant_lists`: entry [g, o, c] is -1 (an empty slot) or a tenant owned by group o, an id from o * 64 to (o + 1) * 64 - 1; the live entries of each [g, o] come first and are distinct; at most 12 are live for each g and o, and one owner has all 12 live in every data group.
All inputs are finite; a program needn't handle non-finite values.
Results may differ from the reference program's by a relative error of at most 0.015.
Values may be sent and summed in bfloat16 or wider, within the bound.
A program may use at most 64 MiB of HBM per device.

```python
import jax
import jax.numpy as jnp
from jax import lax

D = 4096
DQ = 1024
RANK = 16
CAP = 12
TEN_OWN = 64
TOK_DEV = 512
TENANTS = 256
TOKENS = 4096
N_GRP = 4
N_SEQ = 2


def shared_lists(key):
    key_count, key_full, key_pick = jax.random.split(key, 3)
    counts = jax.random.randint(key_count, (N_GRP, N_GRP), 1, CAP + 1)
    full_owner = jax.random.randint(key_full, (), 0, N_GRP)
    counts = jnp.where(jnp.arange(N_GRP)[None, :] == full_owner, CAP, counts)
    pick_keys = jax.random.split(key_pick, N_GRP * N_GRP)
    picks = jax.vmap(lambda k: jax.random.permutation(k, TEN_OWN)[:CAP])(pick_keys).reshape(N_GRP, N_GRP, CAP)
    owner = jnp.arange(N_GRP, dtype=jnp.int32)[None, :, None]
    ids = owner * TEN_OWN + picks.astype(jnp.int32)
    live = jnp.arange(CAP)[None, None, :] < counts[:, :, None]
    return (jnp.where(live, ids, -1).astype(jnp.int32), counts)


def draw_tenant_lists(key, part):
    lists, counts = shared_lists(key)
    return lists


def draw_token_tenant(key, part):
    lists, counts = shared_lists(key)
    key = jax.random.fold_in(key, 7)
    key_owner, key_pos = jax.random.split(key)
    rows = TOK_DEV * N_SEQ
    total = N_GRP * rows
    group = jnp.arange(total) // rows
    owner = jax.random.randint(key_owner, (total,), 0, N_GRP)
    limit = counts[group, owner]
    position = jax.random.randint(key_pos, (total,), 0, limit)
    return lists[group, owner, position].astype(jnp.int32)


def levels(key, extent, pieces, smallest, largest):
    factor_of = 1.0
    for dim, shards_of in pieces:
        steps = jax.random.uniform(jax.random.fold_in(jax.random.fold_in(key, 6), dim), (shards_of,), jnp.float32, smallest / len(pieces), largest / len(pieces))
        factor_of = factor_of * jnp.repeat(jnp.exp(steps), extent[dim] // shards_of).reshape((-1,) + (1,) * (len(extent) - 1 - dim))
    return factor_of


def bell_draw(own_key, shape, deviation, most, pieces=(), kind=jnp.bfloat16):
    result = jax.random.normal(own_key, shape, jnp.float32) * deviation
    if len(pieces) > 0:
        result = levels(own_key, shape, pieces, -0.22, 0.18) * result
    return jnp.clip(result, min=-most, max=most).astype(kind)


def setup_inputs(seed: int = 0) -> dict:
    streams_of = jax.random.split(jax.random.key(seed), 8)
    tokens = bell_draw(streams_of[0], (TOKENS, D), 1.0, 6.0, ((0, 8),))
    base_weight = bell_draw(streams_of[1], (D, DQ), D ** -0.5, 0.09375, ((1, 4),))
    adapter_a = bell_draw(streams_of[2], (TENANTS, RANK, D), D ** -0.5, 0.09375, ((0, 4), (2, 4)))
    adapter_b = bell_draw(streams_of[3], (TENANTS, RANK, DQ), RANK ** -0.5, 1.5, ((0, 4), (2, 4)))
    token_tenant = draw_token_tenant(jax.random.fold_in(streams_of[7], 71), 0)
    tenant_lists = draw_tenant_lists(jax.random.fold_in(streams_of[7], 71), 0)
    cotangent = bell_draw(streams_of[6], (TOKENS, DQ), 0.02, 0.3125, ((0, 8), (1, 4)))
    return dict(tokens=tokens, base_weight=base_weight, adapter_a=adapter_a, adapter_b=adapter_b, token_tenant=token_tenant, tenant_lists=tenant_lists, cotangent=cotangent)


SCALE = 2.0


def device_terms(x, ids, dy, flat, base_weight, adapter_a, adapter_b):
    count = flat.shape[0]
    a_tok = adapter_a[ids].astype(jnp.float32)
    b_tok = adapter_b[ids].astype(jnp.float32)
    xf = x.astype(jnp.float32)
    dyf = dy.astype(jnp.float32)
    low = jnp.einsum('nd,nrd->nr', xf, a_tok).astype(jnp.bfloat16)
    delta = jnp.einsum('nr,nrq->nq', low.astype(jnp.float32), b_tok)
    base = jnp.dot(x, base_weight, preferred_element_type=jnp.float32)
    out = (base + SCALE * delta).astype(jnp.bfloat16)
    back = (SCALE * jnp.einsum('nq,nrq->nr', dyf, b_tok)).astype(jnp.bfloat16)
    slot = jnp.sum(jnp.where(ids[:, None] == flat[None, :], jnp.arange(count, dtype=jnp.int32)[None, :], 0), axis=1).astype(jnp.int32)
    part_a = jax.ops.segment_sum(back.astype(jnp.float32)[:, :, None] * xf[:, None, :], slot, num_segments=count).astype(jnp.bfloat16)
    part_b = (SCALE * jax.ops.segment_sum(low.astype(jnp.float32)[:, :, None] * dyf[:, None, :], slot, num_segments=count)).astype(jnp.bfloat16)
    return out, part_a, part_b


def reference(tokens, base_weight, adapter_a, adapter_b, token_tenant, tenant_lists, cotangent):
    slots = N_GRP * CAP
    x_all = tokens.reshape(N_GRP, N_SEQ, TOK_DEV, D)
    id_all = token_tenant.reshape(N_GRP, N_SEQ, TOK_DEV)
    dy_all = cotangent.reshape(N_GRP, N_SEQ, TOK_DEV, DQ)

    def group_step(carry, inputs):
        grad_a, grad_b = carry
        x_g, ids_g, dy_g, lists_g = inputs
        flat = lists_g.reshape(slots)

        def one_device(inner):
            return device_terms(inner[0], inner[1], inner[2], flat, base_weight, adapter_a, adapter_b)

        out_g, part_a, part_b = lax.map(one_device, (x_g, ids_g, dy_g))
        total_a = jnp.sum(part_a.astype(jnp.float32), axis=0).astype(jnp.bfloat16)
        total_b = jnp.sum(part_b.astype(jnp.float32), axis=0).astype(jnp.bfloat16)
        target = jnp.where(flat >= 0, flat, TENANTS).astype(jnp.int32)
        grad_a = grad_a.at[target].add(total_a.astype(jnp.float32), mode='drop')
        grad_b = grad_b.at[target].add(total_b.astype(jnp.float32), mode='drop')
        return (grad_a, grad_b), out_g

    start = (jnp.zeros((TENANTS, RANK, D), jnp.float32), jnp.zeros((TENANTS, RANK, DQ), jnp.float32))
    (grad_a, grad_b), outs = lax.scan(group_step, start, (x_all, id_all, dy_all, tenant_lists))
    return outs.reshape(TOKENS, DQ), grad_a, grad_b
```

```python
import functools

import jax
import jax.numpy as jnp
from jax import lax
from jax.experimental import pallas as pl
from jax.experimental.pallas import tpu as pltpu
from jax.sharding import PartitionSpec as P

SCALE = 2.0
MESH = pl.DeviceIdType.MESH


def visit_order(groups):
    order = [0]
    for d in range(1, groups // 2 + 1):
        for k in (d, groups - d):
            if k not in order:
                order.append(k)
    return order


def exchange_kernel(
    dims,
    lists_ref,
    tenant_ref,
    tokens_ref,
    weight_ref,
    ad_a_ref,
    ad_b_ref,
    cot_ref,
    proj_ref,
    out_ref,
    xv,
    wv,
    av,
    bv,
    cv,
    fetched,
    sendf,
    ug,
    ugr,
    wide,
    part,
    rsr,
    gsum,
    arr,
    acc,
    load_sem,
    out_sem,
    f_send,
    f_recv,
    fs_send,
    fs_recv,
    tp_send,
    tp_recv,
    rs_send,
    rs_recv,
    z_send,
    z_recv,
    zs_send,
    zs_recv,
):
    G, T, S, share, rank, owned, wa, wb, rows = dims
    R = share * rank
    full = S * R
    me = lax.axis_index("grp")
    tp = lax.axis_index("tp")
    s = lax.axis_index("seq")

    load_a = pltpu.make_async_copy(ad_a_ref, av, load_sem.at[0])
    load_b = pltpu.make_async_copy(ad_b_ref, bv, load_sem.at[1])
    load_a.start()
    load_b.start()
    load_c = pltpu.make_async_copy(cot_ref, cv, load_sem.at[2])
    load_x, load_w = [], []
    for j in range(T):
        at = pl.multiple_of(lax.rem(tp + j, T) * wa, 128)
        load_x.append(
            pltpu.make_async_copy(tokens_ref.at[:, pl.ds(at, wa)], xv.at[j], load_sem.at[3 + j])
        )
        load_w.append(
            pltpu.make_async_copy(weight_ref.at[pl.ds(at, wa), :], wv.at[j], load_sem.at[3 + T + j])
        )
    load_x[0].start()
    load_c.start()
    for j in range(T):
        if j:
            load_x[j].start()
        load_w[j].start()

    barrier = pltpu.get_barrier_semaphore()
    for k in range(1, G):
        pl.semaphore_signal(
            barrier, inc=1, device_id={"grp": lax.rem(me + k, G)}, device_id_type=MESH
        )
    for k in range(1, T):
        pl.semaphore_signal(
            barrier, inc=1, device_id={"tp": lax.rem(tp + k, T)}, device_id_type=MESH
        )
    for k in range(1, S):
        pl.semaphore_signal(
            barrier, inc=1, device_id={"seq": lax.rem(s + k, S)}, device_id_type=MESH
        )

    order = visit_order(G)
    sends = []

    def gather(dst, row, target, slot):
        at = jnp.clip(lists_ref[target, me, slot] - me * owned, 0, owned - 1)
        dst[pl.ds(row, rank), pl.ds(0, wa)] = av[at]
        dst[pl.ds(row, rank), pl.ds(wa, wb)] = bv[at]

    load_a.wait()
    load_b.wait()
    fetch = {}
    first = True
    for k in order[1:]:
        target = lax.rem(me + k, G)
        for j in range(share):
            gather(sendf.at[k - 1], j * rank, target, s * share + j)
        if first:
            pl.semaphore_wait(barrier, (G - 1) + (T - 1) + (S - 1))
            first = False
        fetch[k] = pltpu.make_async_remote_copy(
            src_ref=sendf.at[k - 1],
            dst_ref=fetched.at[k, s],
            send_sem=f_send.at[k],
            recv_sem=f_recv.at[k],
            device_id={"grp": target},
            device_id_type=MESH,
        )
        fetch[k].start()
        sends.append(fetch[k])
    if first:
        pl.semaphore_wait(barrier, (G - 1) + (T - 1) + (S - 1))
    for j in range(S * share):
        gather(fetched.at[0, j // share], (j % share) * rank, me, j)

    ids = tenant_ref[...]

    def members(k):
        owner = lax.rem(me - k + G, G)
        return [ids == lists_ref[me, owner, j] for j in range(S * share)]

    def spread(sem_s, sem_r, k, ref):
        out = []
        for q in range(1, S):
            copy = pltpu.make_async_remote_copy(
                src_ref=ref,
                dst_ref=ref,
                send_sem=sem_s.at[k, q],
                recv_sem=sem_r.at[k, q],
                device_id={"seq": lax.rem(s + q, S)},
                device_id_type=MESH,
            )
            copy.start()
            sends.append(copy)
            out.append(copy)
        return out

    fetch_spread, tp_copies, rs_copies, z_copies, z_spread = {}, {}, {}, {}, {}

    def take_fetch(k):
        fetch[k].wait_recv()
        fetch_spread[k] = spread(fs_send, fs_recv, k, fetched.at[k, s])

    def project(k):
        for copy in fetch_spread.get(k, ()):
            copy.wait_recv()
        tile = fetched[k].reshape(full, wa + wb)
        nt = (((1,), (1,)), ((), ()))
        u = lax.dot_general(tile[:, :wa], xv[0], nt, preferred_element_type=jnp.float32)
        g = lax.dot_general(tile[:, wa:], cv[...], nt, preferred_element_type=jnp.float32)
        us = jnp.zeros((rank, rows), jnp.float32)
        gs = jnp.zeros((rank, rows), jnp.float32)
        for j, m in enumerate(members(k)):
            mm = jnp.broadcast_to(m, (rank, rows))
            us = us + jnp.where(mm, u[j * rank : (j + 1) * rank], 0.0)
            gs = gs + jnp.where(mm, g[j * rank : (j + 1) * rank], 0.0)
        ug[k, pl.ds(0, rank), :] = us.astype(jnp.bfloat16)
        ug[k, pl.ds(rank, rank), :] = gs.astype(jnp.bfloat16)
        tp_copies[k] = []
        for q in range(1, T):
            copy = pltpu.make_async_remote_copy(
                src_ref=ug.at[k],
                dst_ref=ugr.at[k, q - 1],
                send_sem=tp_send.at[k, q],
                recv_sem=tp_recv.at[k, q],
                device_id={"tp": lax.rem(tp + q, T)},
                device_id_type=MESH,
            )
            copy.start()
            sends.append(copy)
            tp_copies[k].append(copy)

    def gradients(k):
        total = ug[k].astype(jnp.float32)
        for q in range(1, T):
            tp_copies[k][q - 1].wait_recv()
            total = total + ugr[k, q - 1].astype(jnp.float32)
        low = total[:rank].astype(jnp.bfloat16).astype(jnp.float32)
        back = (SCALE * total[rank:]).astype(jnp.bfloat16).astype(jnp.float32)
        mem = [jnp.broadcast_to(m, (rank, rows)) for m in members(k)]
        low_wide = jnp.concatenate(
            [jnp.where(m, low, 0.0).astype(jnp.bfloat16) for m in mem], axis=0
        )
        back_wide = jnp.concatenate(
            [jnp.where(m, back, 0.0).astype(jnp.bfloat16) for m in mem], axis=0
        )
        wide[k] = low_wide
        pa = jnp.dot(back_wide, xv[0], preferred_element_type=jnp.float32)
        pb = SCALE * jnp.dot(low_wide, cv[...], preferred_element_type=jnp.float32)
        part[k, :, :, pl.ds(0, wa)] = pa.astype(jnp.bfloat16).reshape(S, R, wa)
        part[k, :, :, pl.ds(wa, wb)] = pb.astype(jnp.bfloat16).reshape(S, R, wb)
        rs_copies[k] = []
        for q in range(1, S):
            peer = lax.rem(s + q, S)
            copy = pltpu.make_async_remote_copy(
                src_ref=part.at[k, peer],
                dst_ref=rsr.at[k, q - 1],
                send_sem=rs_send.at[k, q],
                recv_sem=rs_recv.at[k, q],
                device_id={"seq": peer},
                device_id_type=MESH,
            )
            copy.start()
            sends.append(copy)
            rs_copies[k].append(copy)

    def group_sum(k):
        total = part[k, s].astype(jnp.float32)
        for q in range(1, S):
            rs_copies[k][q - 1].wait_recv()
            total = total + rsr[k, q - 1].astype(jnp.float32)
        if k == 0:
            arr[0, s] = total.astype(jnp.bfloat16)
            z_spread[0] = spread(zs_send, zs_recv, 0, arr.at[0, s])
            return
        gsum[k - 1] = total.astype(jnp.bfloat16)
        z_copies[k] = pltpu.make_async_remote_copy(
            src_ref=gsum.at[k - 1],
            dst_ref=arr.at[k, s],
            send_sem=z_send.at[k],
            recv_sem=z_recv.at[k],
            device_id={"grp": lax.rem(me - k + G, G)},
            device_id_type=MESH,
        )
        z_copies[k].start()
        sends.append(z_copies[k])

    load_x[0].wait()
    load_c.wait()
    project(0)
    for j in range(T):
        if j:
            load_x[j].wait()
        load_w[j].wait()
        term = jnp.dot(xv[j], wv[j], preferred_element_type=jnp.float32)
        acc[...] = term if j == 0 else acc[...] + term
    gradients(0)
    group_sum(0)

    for i in range(1, G, 2):
        pair = order[i : i + 2]
        for k in pair:
            take_fetch(k)
        for k in pair:
            project(k)
        for k in pair:
            gradients(k)
        for k in pair:
            group_sum(k)

    outs = []

    def put_out(k):
        for copy in z_spread[k]:
            copy.wait_recv()
        copy = pltpu.make_async_copy(arr.at[k], out_ref.at[k], out_sem.at[k])
        copy.start()
        outs.append(copy)

    put_out(0)
    low_all = wide[...].reshape(G * full, rows)
    b_all = fetched[:, :, :, pl.ds(wa, wb)].reshape(G * full, wb)
    delta = lax.dot_general(
        low_all, b_all, (((0,), (0,)), ((), ())), preferred_element_type=jnp.float32
    )
    proj_ref[...] = (acc[...] + SCALE * delta).astype(jnp.bfloat16)

    for k in order[1:]:
        z_copies[k].wait_recv()
        z_spread[k] = spread(zs_send, zs_recv, k, arr.at[k, s])
    for k in order[1:]:
        put_out(k)
    for copy in outs:
        copy.wait()
    for copy in sends:
        copy.wait_send()


def owner_kernel(dims, lists_ref, arr_ref, proj_in, proj_ref, ga_ref, gb_ref, buf_a, buf_b, sem):
    G, T, S, share, rank, owned, wa, wb, rows = dims
    me = lax.axis_index("grp")
    slots = S * share
    proj_ref[...] = proj_in[...]
    step = wa // 4 if wa % 512 == 0 else wa
    copies = []
    pieces = [(buf_a, ga_ref, c, c, step) for c in range(0, wa, step)]
    pieces.append((buf_b, gb_ref, 0, wa, wb))
    for n, (buf, out, at, src, size) in enumerate(pieces):
        buf[:, :, pl.ds(at, size)] = jnp.zeros((owned, rank, size), jnp.float32)

        def add(i, _, buf=buf, at=at, src=src, size=size):
            k = i // slots
            c = i - k * slots
            t = lists_ref[lax.rem(me + k, G), me, c]

            @pl.when(t >= 0)
            def _():
                row = t - me * owned
                buf[row, :, pl.ds(at, size)] += arr_ref[i, :, pl.ds(src, size)].astype(jnp.float32)

            return 0

        lax.fori_loop(0, G * slots, add, 0)
        copy = pltpu.make_async_copy(
            buf.at[:, :, pl.ds(at, size)], out.at[:, :, pl.ds(at, size)], sem.at[n]
        )
        copy.start()
        copies.append(copy)
    for copy in copies:
        copy.wait()


def body(tokens, base_weight, adapter_a, adapter_b, token_tenant, tenant_lists, cotangent):
    G = lax.axis_size("grp")
    T = lax.axis_size("tp")
    S = lax.axis_size("seq")
    owned, rank, wa = adapter_a.shape
    wb = adapter_b.shape[2]
    depth = tenant_lists.shape[2]
    rows = tokens.shape[0]
    share = -(-depth // S)
    if share * S != depth:
        tenant_lists = jnp.pad(
            tenant_lists, ((0, 0), (0, 0), (0, share * S - depth)), constant_values=-1
        )
    R = share * rank
    width = wa + wb
    dims = (G, T, S, share, rank, owned, wa, wb, rows)
    bf, f32 = jnp.bfloat16, jnp.float32
    vmem = pl.BlockSpec(memory_space=pltpu.VMEM)
    smem = pl.BlockSpec(memory_space=pltpu.SMEM)
    hbm = pl.BlockSpec(memory_space=pl.ANY)
    dma = pltpu.SemaphoreType.DMA
    proj, arrived = pl.pallas_call(
        functools.partial(exchange_kernel, dims),
        out_shape=(
            jax.ShapeDtypeStruct((rows, wb), bf),
            jax.ShapeDtypeStruct((G, S, R, width), bf),
        ),
        in_specs=[smem, vmem, hbm, hbm, hbm, hbm, hbm],
        out_specs=(vmem, hbm),
        scratch_shapes=[
            pltpu.VMEM((T, rows, wa), bf),
            pltpu.VMEM((T, wa, wb), bf),
            pltpu.VMEM((owned, rank, wa), bf),
            pltpu.VMEM((owned, rank, wb), bf),
            pltpu.VMEM((rows, wb), bf),
            pltpu.VMEM((G, S, R, width), bf),
            pltpu.VMEM((G - 1, R, width), bf),
            pltpu.VMEM((G, 2 * rank, rows), bf),
            pltpu.VMEM((G, T - 1, 2 * rank, rows), bf),
            pltpu.VMEM((G, S * R, rows), bf),
            pltpu.VMEM((G, S, R, width), bf),
            pltpu.VMEM((G, S - 1, R, width), bf),
            pltpu.VMEM((G - 1, R, width), bf),
            pltpu.VMEM((G, S, R, width), bf),
            pltpu.VMEM((rows, wb), f32),
            dma((3 + 2 * T,)),
            dma((G,)),
            dma((G,)),
            dma((G,)),
            dma((G, S)),
            dma((G, S)),
            dma((G, T)),
            dma((G, T)),
            dma((G, S)),
            dma((G, S)),
            dma((G,)),
            dma((G,)),
            dma((G, S)),
            dma((G, S)),
        ],
        compiler_params=pltpu.CompilerParams(
            collective_id=0, has_side_effects=True, vmem_limit_bytes=50 * 2**20
        ),
        name="exchange",
    )(
        tenant_lists,
        token_tenant.reshape(1, rows),
        tokens,
        base_weight,
        adapter_a,
        adapter_b,
        cotangent,
    )
    return pl.pallas_call(
        functools.partial(owner_kernel, dims),
        out_shape=(
            jax.ShapeDtypeStruct((rows, wb), bf),
            jax.ShapeDtypeStruct((owned, rank, wa), f32),
            jax.ShapeDtypeStruct((owned, rank, wb), f32),
        ),
        in_specs=[smem, vmem, vmem],
        out_specs=(vmem, hbm, hbm),
        scratch_shapes=[
            pltpu.VMEM((owned, rank, wa), f32),
            pltpu.VMEM((owned, rank, wb), f32),
            dma((5,)),
        ],
        compiler_params=pltpu.CompilerParams(vmem_limit_bytes=40 * 2**20),
        name="owner_sums",
    )(tenant_lists, arrived.reshape(G * S * share, rank, width), proj)


def solution(mesh):
    return jax.shard_map(
        body,
        mesh=mesh,
        in_specs=(
            P(("grp", "seq"), None),
            P(None, "tp"),
            P("grp", None, "tp"),
            P("grp", None, "tp"),
            P(("grp", "seq")),
            P(),
            P(("grp", "seq"), "tp"),
        ),
        out_specs=(P(("grp", "seq"), "tp"), P("grp", None, "tp"), P("grp", None, "tp")),
        check_vma=False,
    )
```

```python
import functools

import jax
import jax.numpy as jnp
from jax import lax
from jax.experimental import pallas as pl
from jax.experimental.pallas import tpu as pltpu
from jax.sharding import PartitionSpec as P

SCALE = 2.0
MESH = pl.DeviceIdType.MESH


def stages(groups):
    half = groups // 2
    if groups < 2:
        return []
    first = [half] + list(range(1, half))
    return [ks for ks in (first, list(range(half + 1, groups))) if ks]


def partners(me, k, groups):
    if groups & (groups - 1):
        return lax.rem(me + k, groups), lax.rem(me - k + groups, groups)
    other = me
    bit = 1
    while bit < groups:
        if k & bit:
            other = other + bit * (1 - 2 * lax.rem(lax.div(me, bit), 2))
        bit *= 2
    return other, other


def exchange_kernel(
    dims,
    lists_hbm,
    tenant_hbm,
    tokens_ref,
    weight_ref,
    ad_a_ref,
    ad_b_ref,
    cot_ref,
    proj_ref,
    out_ref,
    lists_ref,
    tenant_ref,
    xv,
    wv,
    av,
    bv,
    cv,
    fetched,
    sendf,
    ug,
    ugr,
    wide,
    part,
    rsr,
    gsum,
    arr,
    acc,
    load_sem,
    out_sem,
    f_send,
    f_recv,
    fs_send,
    fs_recv,
    tp_send,
    tp_recv,
    rs_send,
    rs_recv,
    z_send,
    z_recv,
    zs_send,
    zs_recv,
):
    G, T, S, share, rank, owned, wa, wb, rows = dims
    R = share * rank
    full = S * R
    me = lax.axis_index("grp")
    tp = lax.axis_index("tp")
    s = lax.axis_index("seq")

    load_l = pltpu.make_async_copy(lists_hbm, lists_ref, load_sem.at[3 + 2 * T])
    load_t = pltpu.make_async_copy(tenant_hbm, tenant_ref, load_sem.at[4 + 2 * T])
    load_l.start()
    load_a = pltpu.make_async_copy(ad_a_ref, av, load_sem.at[0])
    load_b = pltpu.make_async_copy(ad_b_ref, bv, load_sem.at[1])
    load_a.start()
    load_b.start()
    load_t.start()
    load_c = pltpu.make_async_copy(cot_ref, cv, load_sem.at[2])
    load_x, load_w = [], []
    for j in range(T):
        at = pl.multiple_of(lax.rem(tp + j, T) * wa, 128)
        load_x.append(
            pltpu.make_async_copy(tokens_ref.at[:, pl.ds(at, wa)], xv.at[j], load_sem.at[3 + j])
        )
        load_w.append(
            pltpu.make_async_copy(weight_ref.at[pl.ds(at, wa), :], wv.at[j], load_sem.at[3 + T + j])
        )
    load_x[0].start()
    load_c.start()
    for j in range(T):
        if j:
            load_x[j].start()
        load_w[j].start()

    barrier = pltpu.get_barrier_semaphore()
    for k in range(1, G):
        pl.semaphore_signal(
            barrier, inc=1, device_id={"grp": lax.rem(me + k, G)}, device_id_type=MESH
        )
    for k in range(1, T):
        pl.semaphore_signal(
            barrier, inc=1, device_id={"tp": lax.rem(tp + k, T)}, device_id_type=MESH
        )
    for k in range(1, S):
        pl.semaphore_signal(
            barrier, inc=1, device_id={"seq": lax.rem(s + k, S)}, device_id_type=MESH
        )

    plan = stages(G)
    order = [0] + [k for ks in plan for k in ks]
    late = [k for ks in plan[1:] for k in ks]
    sends = []

    def gather(dst, row, target, slot):
        at = jnp.clip(lists_ref[target, me, slot] - me * owned, 0, owned - 1)
        dst[pl.ds(row, rank), pl.ds(0, wa)] = av[at]
        dst[pl.ds(row, rank), pl.ds(wa, wb)] = bv[at]

    load_l.wait()
    load_a.wait()
    load_b.wait()
    fetch = {}
    first = True
    for k in order[1:]:
        target, _ = partners(me, k, G)
        for j in range(share):
            gather(sendf.at[k - 1], j * rank, target, s * share + j)
        if first:
            pl.semaphore_wait(barrier, (G - 1) + (T - 1) + (S - 1))
            first = False
        fetch[k] = pltpu.make_async_remote_copy(
            src_ref=sendf.at[k - 1],
            dst_ref=fetched.at[k, s],
            send_sem=f_send.at[k],
            recv_sem=f_recv.at[k],
            device_id={"grp": target},
            device_id_type=MESH,
        )
        if k not in late:
            fetch[k].start()
    if first:
        pl.semaphore_wait(barrier, (G - 1) + (T - 1) + (S - 1))
    for j in range(S * share):
        gather(fetched.at[0, j // share], (j % share) * rank, me, j)

    load_t.wait()
    ids = tenant_ref[...]

    def members(k):
        _, owner = partners(me, k, G)
        return [ids == lists_ref[me, owner, j] for j in range(S * share)]

    def spread(sem_s, sem_r, k, ref):
        out = []
        for q in range(1, S):
            copy = pltpu.make_async_remote_copy(
                src_ref=ref,
                dst_ref=ref,
                send_sem=sem_s.at[k, q],
                recv_sem=sem_r.at[k, q],
                device_id={"seq": lax.rem(s + q, S)},
                device_id_type=MESH,
            )
            copy.start()
            sends.append(copy)
            out.append(copy)
        return out

    fetch_spread, tp_copies, rs_copies, z_copies, z_spread = {}, {}, {}, {}, {}

    def take_fetch(k):
        fetch[k].wait_recv()
        fetch_spread[k] = spread(fs_send, fs_recv, k, fetched.at[k, s])

    def project(k):
        for copy in fetch_spread.get(k, ()):
            copy.wait_recv()
        tile = fetched[k].reshape(full, wa + wb)
        nt = (((1,), (1,)), ((), ()))
        u = lax.dot_general(tile[:, :wa], xv[0], nt, preferred_element_type=jnp.float32)
        g = lax.dot_general(tile[:, wa:], cv[...], nt, preferred_element_type=jnp.float32)
        us = jnp.zeros((rank, rows), jnp.float32)
        gs = jnp.zeros((rank, rows), jnp.float32)
        for j, m in enumerate(members(k)):
            mm = jnp.broadcast_to(m, (rank, rows))
            us = us + jnp.where(mm, u[j * rank : (j + 1) * rank], 0.0)
            gs = gs + jnp.where(mm, g[j * rank : (j + 1) * rank], 0.0)
        ug[k, pl.ds(0, rank), :] = us.astype(jnp.bfloat16)
        ug[k, pl.ds(rank, rank), :] = gs.astype(jnp.bfloat16)
        tp_copies[k] = []
        for q in range(1, T):
            copy = pltpu.make_async_remote_copy(
                src_ref=ug.at[k],
                dst_ref=ugr.at[k, q - 1],
                send_sem=tp_send.at[k, q],
                recv_sem=tp_recv.at[k, q],
                device_id={"tp": lax.rem(tp + q, T)},
                device_id_type=MESH,
            )
            copy.start()
            sends.append(copy)
            tp_copies[k].append(copy)

    def gradients(k):
        total = ug[k].astype(jnp.float32)
        for q in range(1, T):
            tp_copies[k][q - 1].wait_recv()
            total = total + ugr[k, q - 1].astype(jnp.float32)
        low = total[:rank].astype(jnp.bfloat16).astype(jnp.float32)
        back = (SCALE * total[rank:]).astype(jnp.bfloat16).astype(jnp.float32)
        mem = [jnp.broadcast_to(m, (rank, rows)) for m in members(k)]
        low_wide = jnp.concatenate(
            [jnp.where(m, low, 0.0).astype(jnp.bfloat16) for m in mem], axis=0
        )
        back_wide = jnp.concatenate(
            [jnp.where(m, back, 0.0).astype(jnp.bfloat16) for m in mem], axis=0
        )
        wide[k] = low_wide
        pa = jnp.dot(back_wide, xv[0], preferred_element_type=jnp.float32)
        pb = SCALE * jnp.dot(low_wide, cv[...], preferred_element_type=jnp.float32)
        part[k, :, :, pl.ds(0, wa)] = pa.astype(jnp.bfloat16).reshape(S, R, wa)
        part[k, :, :, pl.ds(wa, wb)] = pb.astype(jnp.bfloat16).reshape(S, R, wb)
        rs_copies[k] = []
        for q in range(1, S):
            peer = lax.rem(s + q, S)
            copy = pltpu.make_async_remote_copy(
                src_ref=part.at[k, peer],
                dst_ref=rsr.at[k, q - 1],
                send_sem=rs_send.at[k, q],
                recv_sem=rs_recv.at[k, q],
                device_id={"seq": peer},
                device_id_type=MESH,
            )
            copy.start()
            sends.append(copy)
            rs_copies[k].append(copy)

    def group_sum(k):
        total = part[k, s].astype(jnp.float32)
        for q in range(1, S):
            rs_copies[k][q - 1].wait_recv()
            total = total + rsr[k, q - 1].astype(jnp.float32)
        if k == 0:
            arr[0, s] = total.astype(jnp.bfloat16)
            z_spread[0] = spread(zs_send, zs_recv, 0, arr.at[0, s])
            return
        gsum[k - 1] = total.astype(jnp.bfloat16)
        z_copies[k] = pltpu.make_async_remote_copy(
            src_ref=gsum.at[k - 1],
            dst_ref=arr.at[k, s],
            send_sem=z_send.at[k],
            recv_sem=z_recv.at[k],
            device_id={"grp": partners(me, k, G)[1]},
            device_id_type=MESH,
        )
        z_copies[k].start()
        sends.append(z_copies[k])

    load_x[0].wait()
    load_c.wait()
    project(0)
    for j in range(T):
        if j:
            load_x[j].wait()
        load_w[j].wait()
        term = jnp.dot(xv[j], wv[j], preferred_element_type=jnp.float32)
        acc[...] = term if j == 0 else acc[...] + term
    gradients(0)
    group_sum(0)

    for n, ks in enumerate(plan):
        if n == 0:
            fetch[ks[0]].wait_send()
            for k in late:
                fetch[k].start()
            sends.extend(fetch[k] for k in order[1:] if k != ks[0])
        for k in ks:
            take_fetch(k)
        for k in ks:
            project(k)
        for k in ks:
            gradients(k)
        for k in ks:
            group_sum(k)

    outs = []

    def put_out(k):
        for copy in z_spread[k]:
            copy.wait_recv()
        copy = pltpu.make_async_copy(arr.at[k], out_ref.at[k], out_sem.at[k])
        copy.start()
        outs.append(copy)

    put_out(0)
    low_all = wide[...].reshape(G * full, rows)
    b_all = fetched[:, :, :, pl.ds(wa, wb)].reshape(G * full, wb)
    delta = lax.dot_general(
        low_all, b_all, (((0,), (0,)), ((), ())), preferred_element_type=jnp.float32
    )
    proj_ref[...] = (acc[...] + SCALE * delta).astype(jnp.bfloat16)

    for k in order[1:]:
        z_copies[k].wait_recv()
        z_spread[k] = spread(zs_send, zs_recv, k, arr.at[k, s])
    for k in order[1:]:
        put_out(k)
    for copy in outs:
        copy.wait()
    for copy in sends:
        copy.wait_send()


def owner_kernel(
    dims,
    lists_hbm,
    arr_hbm,
    proj_in,
    proj_ref,
    ga_ref,
    gb_ref,
    lists_ref,
    arr_ref,
    buf_a,
    buf_b,
    sem,
    load_sem,
):
    G, T, S, share, rank, owned, wa, wb, rows = dims
    me = lax.axis_index("grp")
    slots = S * share
    load_l = pltpu.make_async_copy(lists_hbm, lists_ref, load_sem.at[0])
    load_l.start()
    load_arr = pltpu.make_async_copy(arr_hbm, arr_ref, load_sem.at[1])
    load_arr.start()
    copies = [pltpu.make_async_copy(proj_in, proj_ref, load_sem.at[2])]
    copies[0].start()
    step = wa // 2 if wa % 256 == 0 else wa
    pieces = [(buf_a, ga_ref, c, c, step) for c in range(0, wa, step)]
    pieces.append((buf_b, gb_ref, 0, wa, wb))
    buf_a[...] = jnp.zeros_like(buf_a)
    buf_b[...] = jnp.zeros_like(buf_b)
    load_l.wait()
    targets = []
    for k in range(G):
        group, _ = partners(me, k, G)
        for c in range(slots):
            t = lists_ref[group, me, c]
            targets.append(jnp.where(t >= 0, t - me * owned, owned))
    load_arr.wait()
    for n, (buf, out, at, src, size) in enumerate(pieces):
        for i, row in enumerate(targets):
            buf[row, :, at : at + size] += arr_ref[i, :, src : src + size].astype(jnp.float32)
        copy = pltpu.make_async_copy(
            buf.at[pl.ds(0, owned), :, pl.ds(at, size)], out.at[:, :, pl.ds(at, size)], sem.at[n]
        )
        copy.start()
        copies.append(copy)
    for copy in copies:
        copy.wait()


def body(tokens, base_weight, adapter_a, adapter_b, token_tenant, tenant_lists, cotangent):
    G = lax.axis_size("grp")
    T = lax.axis_size("tp")
    S = lax.axis_size("seq")
    owned, rank, wa = adapter_a.shape
    wb = adapter_b.shape[2]
    depth = tenant_lists.shape[2]
    rows = tokens.shape[0]
    share = -(-depth // S)
    if share * S != depth:
        tenant_lists = jnp.pad(
            tenant_lists, ((0, 0), (0, 0), (0, share * S - depth)), constant_values=-1
        )
    R = share * rank
    width = wa + wb
    slots = share * S
    dims = (G, T, S, share, rank, owned, wa, wb, rows)
    bf, f32 = jnp.bfloat16, jnp.float32
    vmem = pl.BlockSpec(memory_space=pltpu.VMEM)
    hbm = pl.BlockSpec(memory_space=pl.ANY)
    dma = pltpu.SemaphoreType.DMA
    proj, arrived = pl.pallas_call(
        functools.partial(exchange_kernel, dims),
        out_shape=(
            jax.ShapeDtypeStruct((rows, wb), bf),
            jax.ShapeDtypeStruct((G, S, R, width), bf),
        ),
        in_specs=[hbm] * 7,
        out_specs=(vmem, hbm),
        scratch_shapes=[
            pltpu.SMEM((G, G, share * S), jnp.int32),
            pltpu.VMEM((1, rows), jnp.int32),
            pltpu.VMEM((T, rows, wa), bf),
            pltpu.VMEM((T, wa, wb), bf),
            pltpu.VMEM((owned, rank, wa), bf),
            pltpu.VMEM((owned, rank, wb), bf),
            pltpu.VMEM((rows, wb), bf),
            pltpu.VMEM((G, S, R, width), bf),
            pltpu.VMEM((G - 1, R, width), bf),
            pltpu.VMEM((G, 2 * rank, rows), bf),
            pltpu.VMEM((G, T - 1, 2 * rank, rows), bf),
            pltpu.VMEM((G, S * R, rows), bf),
            pltpu.VMEM((G, S, R, width), bf),
            pltpu.VMEM((G, S - 1, R, width), bf),
            pltpu.VMEM((G - 1, R, width), bf),
            pltpu.VMEM((G, S, R, width), bf),
            pltpu.VMEM((rows, wb), f32),
            dma((5 + 2 * T,)),
            dma((G,)),
            dma((G,)),
            dma((G,)),
            dma((G, S)),
            dma((G, S)),
            dma((G, T)),
            dma((G, T)),
            dma((G, S)),
            dma((G, S)),
            dma((G,)),
            dma((G,)),
            dma((G, S)),
            dma((G, S)),
        ],
        compiler_params=pltpu.CompilerParams(
            collective_id=0, has_side_effects=True, vmem_limit_bytes=64 * 2**20
        ),
        name="exchange",
    )(
        tenant_lists,
        token_tenant.reshape(1, rows),
        tokens,
        base_weight,
        adapter_a,
        adapter_b,
        cotangent,
    )
    return pl.pallas_call(
        functools.partial(owner_kernel, dims),
        out_shape=(
            jax.ShapeDtypeStruct((rows, wb), bf),
            jax.ShapeDtypeStruct((owned, rank, wa), f32),
            jax.ShapeDtypeStruct((owned, rank, wb), f32),
        ),
        in_specs=[hbm, hbm, hbm],
        out_specs=(hbm, hbm, hbm),
        scratch_shapes=[
            pltpu.SMEM((G, G, slots), jnp.int32),
            pltpu.VMEM((G * slots, rank, width), bf),
            pltpu.VMEM((owned + 1, rank, wa), f32),
            pltpu.VMEM((owned + 1, rank, wb), f32),
            dma((3,)),
            dma((3,)),
        ],
        compiler_params=pltpu.CompilerParams(vmem_limit_bytes=64 * 2**20),
        name="owner_sums",
    )(tenant_lists, arrived.reshape(G * S * share, rank, width), proj)


def solution(mesh):
    return jax.shard_map(
        body,
        mesh=mesh,
        in_specs=(
            P(("grp", "seq"), None),
            P(None, "tp"),
            P("grp", None, "tp"),
            P("grp", None, "tp"),
            P(("grp", "seq")),
            P(),
            P(("grp", "seq"), "tp"),
        ),
        out_specs=(P(("grp", "seq"), "tp"), P("grp", None, "tp"), P("grp", None, "tp")),
        check_vma=False,
    )
```

```python
import functools

import jax
import jax.numpy as jnp
from jax import lax
from jax.experimental import pallas as pl
from jax.experimental.pallas import tpu as pltpu
from jax.sharding import PartitionSpec as P

SCALE = 2.0
MESH = pl.DeviceIdType.MESH


def stages(groups):
    half = groups // 2
    if groups < 2:
        return []
    first = [half] + list(range(1, half))
    return [ks for ks in (first, list(range(half + 1, groups))) if ks]


def partners(me, k, groups):
    if groups & (groups - 1):
        return lax.rem(me + k, groups), lax.rem(me - k + groups, groups)
    other = me
    bit = 1
    while bit < groups:
        if k & bit:
            other = other + bit * (1 - 2 * lax.rem(lax.div(me, bit), 2))
        bit *= 2
    return other, other


def exchange_kernel(
    dims,
    lists_hbm,
    tenant_hbm,
    tokens_ref,
    weight_ref,
    ad_a_ref,
    ad_b_ref,
    cot_ref,
    proj_ref,
    out_ref,
    lists_ref,
    tenant_ref,
    xv,
    wv,
    av,
    bv,
    cv,
    fetched,
    sendf,
    ug,
    ugr,
    wide,
    part,
    rsr,
    gsum,
    arr,
    acc,
    load_sem,
    out_sem,
    f_send,
    f_recv,
    fs_send,
    fs_recv,
    tp_send,
    tp_recv,
    rs_send,
    rs_recv,
    z_send,
    z_recv,
    zs_send,
    zs_recv,
):
    G, T, S, share, rank, owned, wa, wb, rows = dims
    R = share * rank
    full = S * R
    me = lax.axis_index("grp")
    tp = lax.axis_index("tp")
    s = lax.axis_index("seq")

    load_l = pltpu.make_async_copy(lists_hbm, lists_ref, load_sem.at[3 + 2 * T])
    load_t = pltpu.make_async_copy(tenant_hbm, tenant_ref, load_sem.at[4 + 2 * T])
    load_l.start()
    load_a = pltpu.make_async_copy(ad_a_ref, av, load_sem.at[0])
    load_b = pltpu.make_async_copy(ad_b_ref, bv, load_sem.at[1])
    load_a.start()
    load_b.start()
    load_t.start()
    load_c = pltpu.make_async_copy(cot_ref, cv, load_sem.at[2])
    load_x, load_w = [], []
    for j in range(T):
        at = pl.multiple_of(lax.rem(tp + j, T) * wa, 128)
        load_x.append(
            pltpu.make_async_copy(tokens_ref.at[:, pl.ds(at, wa)], xv.at[j], load_sem.at[3 + j])
        )
        load_w.append(
            pltpu.make_async_copy(weight_ref.at[pl.ds(at, wa), :], wv.at[j], load_sem.at[3 + T + j])
        )
    load_x[0].start()
    load_c.start()
    for j in range(T):
        if j:
            load_x[j].start()
        load_w[j].start()

    barrier = pltpu.get_barrier_semaphore()
    for k in range(1, G):
        pl.semaphore_signal(
            barrier, inc=1, device_id={"grp": lax.rem(me + k, G)}, device_id_type=MESH
        )
    for k in range(1, T):
        pl.semaphore_signal(
            barrier, inc=1, device_id={"tp": lax.rem(tp + k, T)}, device_id_type=MESH
        )
    for k in range(1, S):
        pl.semaphore_signal(
            barrier, inc=1, device_id={"seq": lax.rem(s + k, S)}, device_id_type=MESH
        )

    plan = stages(G)
    order = [0] + [k for ks in plan for k in ks]
    late = [k for ks in plan[1:] for k in ks]
    sends = []

    def gather(dst, row, target, slot):
        at = jnp.clip(lists_ref[target, me, slot] - me * owned, 0, owned - 1)
        dst[pl.ds(row, rank), pl.ds(0, wa)] = av[at]
        dst[pl.ds(row, rank), pl.ds(wa, wb)] = bv[at]

    load_l.wait()
    load_a.wait()
    load_b.wait()
    fetch = {}
    first = True
    for k in order[1:]:
        target, _ = partners(me, k, G)
        for j in range(share):
            gather(sendf.at[k - 1], j * rank, target, s * share + j)
        if first:
            pl.semaphore_wait(barrier, (G - 1) + (T - 1) + (S - 1))
            first = False
        fetch[k] = pltpu.make_async_remote_copy(
            src_ref=sendf.at[k - 1],
            dst_ref=fetched.at[k, s],
            send_sem=f_send.at[k],
            recv_sem=f_recv.at[k],
            device_id={"grp": target},
            device_id_type=MESH,
        )
        if k not in late:
            fetch[k].start()
    if first:
        pl.semaphore_wait(barrier, (G - 1) + (T - 1) + (S - 1))
    for j in range(S * share):
        gather(fetched.at[0, j // share], (j % share) * rank, me, j)

    load_t.wait()
    ids = tenant_ref[...]

    def members(k):
        _, owner = partners(me, k, G)
        return [ids == lists_ref[me, owner, j] for j in range(S * share)]

    def spread(sem_s, sem_r, k, ref, h=0):
        out = []
        for q in range(1, S):
            copy = pltpu.make_async_remote_copy(
                src_ref=ref,
                dst_ref=ref,
                send_sem=sem_s.at[k, q, h],
                recv_sem=sem_r.at[k, q, h],
                device_id={"seq": lax.rem(s + q, S)},
                device_id_type=MESH,
            )
            copy.start()
            sends.append(copy)
            out.append(copy)
        return out

    def halves(k):
        if k in late and R % 32 == 0:
            return [(0, pl.ds(0, R // 2)), (1, pl.ds(R // 2, R // 2))]
        return [(0, pl.ds(0, R))]

    fetch_spread, tp_copies, rs_copies, z_copies, z_spread = {}, {}, {}, {}, {}

    def take_fetch(k):
        fetch[k].wait_recv()
        fetch_spread[k] = spread(fs_send, fs_recv, k, fetched.at[k, s])

    def project(k):
        for copy in fetch_spread.get(k, ()):
            copy.wait_recv()
        tile = fetched[k].reshape(full, wa + wb)
        nt = (((1,), (1,)), ((), ()))
        u = lax.dot_general(tile[:, :wa], xv[0], nt, preferred_element_type=jnp.float32)
        g = lax.dot_general(tile[:, wa:], cv[...], nt, preferred_element_type=jnp.float32)
        us = jnp.zeros((rank, rows), jnp.float32)
        gs = jnp.zeros((rank, rows), jnp.float32)
        for j, m in enumerate(members(k)):
            mm = jnp.broadcast_to(m, (rank, rows))
            us = us + jnp.where(mm, u[j * rank : (j + 1) * rank], 0.0)
            gs = gs + jnp.where(mm, g[j * rank : (j + 1) * rank], 0.0)
        ug[k, pl.ds(0, rank), :] = us.astype(jnp.bfloat16)
        ug[k, pl.ds(rank, rank), :] = gs.astype(jnp.bfloat16)
        tp_copies[k] = []
        for q in range(1, T):
            copy = pltpu.make_async_remote_copy(
                src_ref=ug.at[k],
                dst_ref=ugr.at[k, q - 1],
                send_sem=tp_send.at[k, q],
                recv_sem=tp_recv.at[k, q],
                device_id={"tp": lax.rem(tp + q, T)},
                device_id_type=MESH,
            )
            copy.start()
            sends.append(copy)
            tp_copies[k].append(copy)

    def gradients(k):
        total = ug[k].astype(jnp.float32)
        for q in range(1, T):
            tp_copies[k][q - 1].wait_recv()
            total = total + ugr[k, q - 1].astype(jnp.float32)
        low = total[:rank].astype(jnp.bfloat16).astype(jnp.float32)
        back = (SCALE * total[rank:]).astype(jnp.bfloat16).astype(jnp.float32)
        mem = [jnp.broadcast_to(m, (rank, rows)) for m in members(k)]
        low_wide = jnp.concatenate(
            [jnp.where(m, low, 0.0).astype(jnp.bfloat16) for m in mem], axis=0
        )
        back_wide = jnp.concatenate(
            [jnp.where(m, back, 0.0).astype(jnp.bfloat16) for m in mem], axis=0
        )
        wide[k] = low_wide
        pa = jnp.dot(back_wide, xv[0], preferred_element_type=jnp.float32)
        pb = SCALE * jnp.dot(low_wide, cv[...], preferred_element_type=jnp.float32)
        part[k, :, :, pl.ds(0, wa)] = pa.astype(jnp.bfloat16).reshape(S, R, wa)
        part[k, :, :, pl.ds(wa, wb)] = pb.astype(jnp.bfloat16).reshape(S, R, wb)
        rs_copies[k] = []
        for q in range(1, S):
            peer = lax.rem(s + q, S)
            copy = pltpu.make_async_remote_copy(
                src_ref=part.at[k, peer],
                dst_ref=rsr.at[k, q - 1],
                send_sem=rs_send.at[k, q],
                recv_sem=rs_recv.at[k, q],
                device_id={"seq": peer},
                device_id_type=MESH,
            )
            copy.start()
            sends.append(copy)
            rs_copies[k].append(copy)

    def group_sum(k):
        total = part[k, s].astype(jnp.float32)
        for q in range(1, S):
            rs_copies[k][q - 1].wait_recv()
            total = total + rsr[k, q - 1].astype(jnp.float32)
        if k == 0:
            arr[0, s] = total.astype(jnp.bfloat16)
            z_spread[0] = spread(zs_send, zs_recv, 0, arr.at[0, s])
            return
        gsum[k - 1] = total.astype(jnp.bfloat16)
        z_copies[k] = []
        for h, span in halves(k):
            copy = pltpu.make_async_remote_copy(
                src_ref=gsum.at[k - 1, span],
                dst_ref=arr.at[k, s, span],
                send_sem=z_send.at[k, h],
                recv_sem=z_recv.at[k, h],
                device_id={"grp": partners(me, k, G)[1]},
                device_id_type=MESH,
            )
            copy.start()
            sends.append(copy)
            z_copies[k].append(copy)

    load_x[0].wait()
    load_c.wait()
    project(0)
    for j in range(T):
        if j:
            load_x[j].wait()
        load_w[j].wait()
        term = jnp.dot(xv[j], wv[j], preferred_element_type=jnp.float32)
        acc[...] = term if j == 0 else acc[...] + term
    gradients(0)
    group_sum(0)

    for n, ks in enumerate(plan):
        if n == 0:
            fetch[ks[0]].wait_send()
            for k in late:
                fetch[k].start()
            sends.extend(fetch[k] for k in order[1:] if k != ks[0])
        for k in ks:
            take_fetch(k)
        for k in ks:
            project(k)
        for k in ks:
            gradients(k)
        for k in ks:
            group_sum(k)

    outs = []

    def put_out(k):
        for copy in z_spread[k]:
            copy.wait_recv()
        copy = pltpu.make_async_copy(arr.at[k], out_ref.at[k], out_sem.at[k])
        copy.start()
        outs.append(copy)

    put_out(0)
    low_all = wide[...].reshape(G * full, rows)
    b_all = fetched[:, :, :, pl.ds(wa, wb)].reshape(G * full, wb)
    delta = lax.dot_general(
        low_all, b_all, (((0,), (0,)), ((), ())), preferred_element_type=jnp.float32
    )
    proj_ref[...] = (acc[...] + SCALE * delta).astype(jnp.bfloat16)

    for k in order[1:]:
        z_spread[k] = []
        for h, span in halves(k):
            z_copies[k][h].wait_recv()
            z_spread[k] += spread(zs_send, zs_recv, k, arr.at[k, s, span], h)
        if k not in late:
            put_out(k)
    for k in late:
        put_out(k)
    for copy in outs:
        copy.wait()
    for copy in sends:
        copy.wait_send()


def owner_kernel(
    dims,
    lists_hbm,
    arr_hbm,
    proj_in,
    proj_ref,
    ga_ref,
    gb_ref,
    lists_ref,
    arr_ref,
    buf_a,
    buf_b,
    proj_v,
    sem,
    load_sem,
):
    G, T, S, share, rank, owned, wa, wb, rows = dims
    me = lax.axis_index("grp")
    slots = S * share
    load_l = pltpu.make_async_copy(lists_hbm, lists_ref, load_sem.at[0])
    load_l.start()
    load_arr = pltpu.make_async_copy(arr_hbm, arr_ref, load_sem.at[1])
    load_arr.start()
    load_p = pltpu.make_async_copy(proj_in, proj_v, load_sem.at[2])
    load_p.start()
    buf_a[...] = jnp.zeros_like(buf_a)
    buf_b[...] = jnp.zeros_like(buf_b)
    load_l.wait()
    targets = []
    for k in range(G):
        group, _ = partners(me, k, G)
        for c in range(slots):
            t = lists_ref[group, me, c]
            targets.append(jnp.where(t >= 0, t - me * owned, owned))
    load_p.wait()
    copies = [pltpu.make_async_copy(proj_v, proj_ref, sem.at[0])]
    copies[0].start()
    load_arr.wait()
    for i, row in enumerate(targets):
        buf_a[row] += arr_ref[i, :, :wa].astype(jnp.float32)
        buf_b[row] += arr_ref[i, :, wa:].astype(jnp.float32)
    for n, (buf, out) in enumerate(((buf_a, ga_ref), (buf_b, gb_ref))):
        copies.append(pltpu.make_async_copy(buf.at[pl.ds(0, owned)], out, sem.at[n + 1]))
        copies[-1].start()
    for copy in copies:
        copy.wait()


def body(tokens, base_weight, adapter_a, adapter_b, token_tenant, tenant_lists, cotangent):
    G = lax.axis_size("grp")
    T = lax.axis_size("tp")
    S = lax.axis_size("seq")
    owned, rank, wa = adapter_a.shape
    wb = adapter_b.shape[2]
    depth = tenant_lists.shape[2]
    rows = tokens.shape[0]
    share = -(-depth // S)
    if share * S != depth:
        tenant_lists = jnp.pad(
            tenant_lists, ((0, 0), (0, 0), (0, share * S - depth)), constant_values=-1
        )
    R = share * rank
    width = wa + wb
    slots = share * S
    dims = (G, T, S, share, rank, owned, wa, wb, rows)
    bf, f32 = jnp.bfloat16, jnp.float32
    vmem = pl.BlockSpec(memory_space=pltpu.VMEM)
    hbm = pl.BlockSpec(memory_space=pl.ANY)
    dma = pltpu.SemaphoreType.DMA
    proj, arrived = pl.pallas_call(
        functools.partial(exchange_kernel, dims),
        out_shape=(
            jax.ShapeDtypeStruct((rows, wb), bf),
            jax.ShapeDtypeStruct((G, S, R, width), bf),
        ),
        in_specs=[hbm] * 7,
        out_specs=(vmem, hbm),
        scratch_shapes=[
            pltpu.SMEM((G, G, share * S), jnp.int32),
            pltpu.VMEM((1, rows), jnp.int32),
            pltpu.VMEM((T, rows, wa), bf),
            pltpu.VMEM((T, wa, wb), bf),
            pltpu.VMEM((owned, rank, wa), bf),
            pltpu.VMEM((owned, rank, wb), bf),
            pltpu.VMEM((rows, wb), bf),
            pltpu.VMEM((G, S, R, width), bf),
            pltpu.VMEM((G - 1, R, width), bf),
            pltpu.VMEM((G, 2 * rank, rows), bf),
            pltpu.VMEM((G, T - 1, 2 * rank, rows), bf),
            pltpu.VMEM((G, S * R, rows), bf),
            pltpu.VMEM((G, S, R, width), bf),
            pltpu.VMEM((G, S - 1, R, width), bf),
            pltpu.VMEM((G - 1, R, width), bf),
            pltpu.VMEM((G, S, R, width), bf),
            pltpu.VMEM((rows, wb), f32),
            dma((5 + 2 * T,)),
            dma((G,)),
            dma((G,)),
            dma((G,)),
            dma((G, S, 1)),
            dma((G, S, 1)),
            dma((G, T)),
            dma((G, T)),
            dma((G, S)),
            dma((G, S)),
            dma((G, 2)),
            dma((G, 2)),
            dma((G, S, 2)),
            dma((G, S, 2)),
        ],
        compiler_params=pltpu.CompilerParams(
            collective_id=0, has_side_effects=True, vmem_limit_bytes=64 * 2**20
        ),
        name="exchange",
    )(
        tenant_lists,
        token_tenant.reshape(1, rows),
        tokens,
        base_weight,
        adapter_a,
        adapter_b,
        cotangent,
    )
    return pl.pallas_call(
        functools.partial(owner_kernel, dims),
        out_shape=(
            jax.ShapeDtypeStruct((rows, wb), bf),
            jax.ShapeDtypeStruct((owned, rank, wa), f32),
            jax.ShapeDtypeStruct((owned, rank, wb), f32),
        ),
        in_specs=[hbm, hbm, hbm],
        out_specs=(hbm, hbm, hbm),
        scratch_shapes=[
            pltpu.SMEM((G, G, slots), jnp.int32),
            pltpu.VMEM((G * slots, rank, width), bf),
            pltpu.VMEM((owned + 1, rank, wa), f32),
            pltpu.VMEM((owned + 1, rank, wb), f32),
            pltpu.VMEM((rows, wb), bf),
            dma((3,)),
            dma((3,)),
        ],
        compiler_params=pltpu.CompilerParams(vmem_limit_bytes=64 * 2**20),
        name="owner_sums",
    )(tenant_lists, arrived.reshape(G * S * share, rank, width), proj)


def solution(mesh):
    return jax.shard_map(
        body,
        mesh=mesh,
        in_specs=(
            P(("grp", "seq"), None),
            P(None, "tp"),
            P("grp", None, "tp"),
            P("grp", None, "tp"),
            P(("grp", "seq")),
            P(),
            P(("grp", "seq"), "tp"),
        ),
        out_specs=(P(("grp", "seq"), "tp"), P("grp", None, "tp"), P("grp", None, "tp")),
        check_vma=False,
    )
```

```python
import functools

import jax
import jax.numpy as jnp
from jax import lax
from jax.experimental import pallas as pl
from jax.experimental.pallas import tpu as pltpu
from jax.sharding import PartitionSpec as P

SCALE = 2.0
MESH = pl.DeviceIdType.MESH


def stages(groups):
    half = groups // 2
    if groups < 2:
        return []
    first = [half] + list(range(1, half))
    return [ks for ks in (first, list(range(half + 1, groups))) if ks]


def partners(me, k, groups):
    if groups & (groups - 1):
        return lax.rem(me + k, groups), lax.rem(me - k + groups, groups)
    other = me
    bit = 1
    while bit < groups:
        if k & bit:
            other = other + bit * (1 - 2 * lax.rem(lax.div(me, bit), 2))
        bit *= 2
    return other, other


def exchange_kernel(
    dims,
    lists_hbm,
    tenant_hbm,
    tokens_ref,
    weight_ref,
    ad_a_ref,
    ad_b_ref,
    cot_ref,
    proj_ref,
    out_ref,
    lists_ref,
    tenant_ref,
    xv,
    wv,
    av,
    bv,
    cv,
    fetched,
    sendf,
    ug,
    ugr,
    wide,
    part,
    rsr,
    gsum,
    arr,
    acc,
    load_sem,
    out_sem,
    f_send,
    f_recv,
    fs_send,
    fs_recv,
    tp_send,
    tp_recv,
    rs_send,
    rs_recv,
    z_send,
    z_recv,
    zs_send,
    zs_recv,
):
    G, T, S, share, rank, owned, wa, wb, rows = dims
    R = share * rank
    full = S * R
    me = lax.axis_index("grp")
    tp = lax.axis_index("tp")
    s = lax.axis_index("seq")

    load_l = pltpu.make_async_copy(lists_hbm, lists_ref, load_sem.at[3 + 2 * T])
    load_t = pltpu.make_async_copy(tenant_hbm, tenant_ref, load_sem.at[4 + 2 * T])
    load_l.start()
    load_a = pltpu.make_async_copy(ad_a_ref, av, load_sem.at[0])
    load_b = pltpu.make_async_copy(ad_b_ref, bv, load_sem.at[1])
    load_a.start()
    load_b.start()
    load_t.start()
    load_c = pltpu.make_async_copy(cot_ref, cv, load_sem.at[2])
    load_x, load_w = [], []
    for j in range(T):
        at = pl.multiple_of(lax.rem(tp + j, T) * wa, 128)
        load_x.append(
            pltpu.make_async_copy(tokens_ref.at[:, pl.ds(at, wa)], xv.at[j], load_sem.at[3 + j])
        )
        load_w.append(
            pltpu.make_async_copy(weight_ref.at[pl.ds(at, wa), :], wv.at[j], load_sem.at[3 + T + j])
        )
    load_x[0].start()
    load_c.start()
    for j in range(T):
        if j:
            load_x[j].start()
        load_w[j].start()

    barrier = pltpu.get_barrier_semaphore()
    for k in range(1, G):
        pl.semaphore_signal(
            barrier, inc=1, device_id={"grp": lax.rem(me + k, G)}, device_id_type=MESH
        )
    for k in range(1, T):
        pl.semaphore_signal(
            barrier, inc=1, device_id={"tp": lax.rem(tp + k, T)}, device_id_type=MESH
        )
    for k in range(1, S):
        pl.semaphore_signal(
            barrier, inc=1, device_id={"seq": lax.rem(s + k, S)}, device_id_type=MESH
        )

    plan = stages(G)
    order = [0] + [k for ks in plan for k in ks]
    late = [k for ks in plan[1:] for k in ks]
    sends = []

    def gather(dst, row, target, slot):
        at = jnp.clip(lists_ref[target, me, slot] - me * owned, 0, owned - 1)
        dst[pl.ds(row, rank), pl.ds(0, wa)] = av[at]
        dst[pl.ds(row, rank), pl.ds(wa, wb)] = bv[at]

    load_l.wait()
    load_a.wait()
    load_b.wait()
    fetch = {}
    first = True
    for k in order[1:]:
        target, _ = partners(me, k, G)
        for j in range(share):
            gather(sendf.at[k - 1], j * rank, target, s * share + j)
        if first:
            pl.semaphore_wait(barrier, (G - 1) + (T - 1) + (S - 1))
            first = False
        fetch[k] = pltpu.make_async_remote_copy(
            src_ref=sendf.at[k - 1],
            dst_ref=fetched.at[k, s],
            send_sem=f_send.at[k],
            recv_sem=f_recv.at[k],
            device_id={"grp": target},
            device_id_type=MESH,
        )
        if k not in late:
            fetch[k].start()
    if first:
        pl.semaphore_wait(barrier, (G - 1) + (T - 1) + (S - 1))
    for j in range(S * share):
        gather(fetched.at[0, j // share], (j % share) * rank, me, j)

    load_t.wait()
    ids = tenant_ref[...]

    def members(k):
        _, owner = partners(me, k, G)
        return [ids == lists_ref[me, owner, j] for j in range(S * share)]

    def spread(sem_s, sem_r, k, ref, h=0):
        out = []
        for q in range(1, S):
            copy = pltpu.make_async_remote_copy(
                src_ref=ref,
                dst_ref=ref,
                send_sem=sem_s.at[k, q, h],
                recv_sem=sem_r.at[k, q, h],
                device_id={"seq": lax.rem(s + q, S)},
                device_id_type=MESH,
            )
            copy.start()
            sends.append(copy)
            out.append(copy)
        return out

    def halves(k):
        if k in late and R % 32 == 0:
            return [(0, pl.ds(0, R // 2)), (1, pl.ds(R // 2, R // 2))]
        return [(0, pl.ds(0, R))]

    fetch_spread, tp_copies, rs_copies, z_copies, z_spread = {}, {}, {}, {}, {}

    def take_fetch(k):
        fetch[k].wait_recv()
        fetch_spread[k] = spread(fs_send, fs_recv, k, fetched.at[k, s])

    def project(k):
        for copy in fetch_spread.get(k, ()):
            copy.wait_recv()
        tile = fetched[k].reshape(full, wa + wb)
        nt = (((1,), (1,)), ((), ()))
        u = lax.dot_general(tile[:, :wa], xv[0], nt, preferred_element_type=jnp.float32)
        g = lax.dot_general(tile[:, wa:], cv[...], nt, preferred_element_type=jnp.float32)
        us = jnp.zeros((rank, rows), jnp.float32)
        gs = jnp.zeros((rank, rows), jnp.float32)
        for j, m in enumerate(members(k)):
            mm = jnp.broadcast_to(m, (rank, rows))
            us = us + jnp.where(mm, u[j * rank : (j + 1) * rank], 0.0)
            gs = gs + jnp.where(mm, g[j * rank : (j + 1) * rank], 0.0)
        ug[k, pl.ds(0, rank), :] = us.astype(jnp.bfloat16)
        ug[k, pl.ds(rank, rank), :] = gs.astype(jnp.bfloat16)
        tp_copies[k] = []
        for q in range(1, T):
            copy = pltpu.make_async_remote_copy(
                src_ref=ug.at[k],
                dst_ref=ugr.at[k, q - 1],
                send_sem=tp_send.at[k, q],
                recv_sem=tp_recv.at[k, q],
                device_id={"tp": lax.rem(tp + q, T)},
                device_id_type=MESH,
            )
            copy.start()
            sends.append(copy)
            tp_copies[k].append(copy)

    def gradients(k):
        total = ug[k].astype(jnp.float32)
        for q in range(1, T):
            tp_copies[k][q - 1].wait_recv()
            total = total + ugr[k, q - 1].astype(jnp.float32)
        low = total[:rank].astype(jnp.bfloat16).astype(jnp.float32)
        back = (SCALE * total[rank:]).astype(jnp.bfloat16).astype(jnp.float32)
        mem = [jnp.broadcast_to(m, (rank, rows)) for m in members(k)]
        low_wide = jnp.concatenate(
            [jnp.where(m, low, 0.0).astype(jnp.bfloat16) for m in mem], axis=0
        )
        back_wide = jnp.concatenate(
            [jnp.where(m, back, 0.0).astype(jnp.bfloat16) for m in mem], axis=0
        )
        wide[k] = low_wide
        pa = jnp.dot(back_wide, xv[0], preferred_element_type=jnp.float32)
        pb = SCALE * jnp.dot(low_wide, cv[...], preferred_element_type=jnp.float32)
        part[k, :, :, pl.ds(0, wa)] = pa.astype(jnp.bfloat16).reshape(S, R, wa)
        part[k, :, :, pl.ds(wa, wb)] = pb.astype(jnp.bfloat16).reshape(S, R, wb)
        rs_copies[k] = []
        for q in range(1, S):
            peer = lax.rem(s + q, S)
            copy = pltpu.make_async_remote_copy(
                src_ref=part.at[k, peer],
                dst_ref=rsr.at[k, q - 1],
                send_sem=rs_send.at[k, q],
                recv_sem=rs_recv.at[k, q],
                device_id={"seq": peer},
                device_id_type=MESH,
            )
            copy.start()
            sends.append(copy)
            rs_copies[k].append(copy)

    def group_sum(k):
        total = part[k, s].astype(jnp.float32)
        for q in range(1, S):
            rs_copies[k][q - 1].wait_recv()
            total = total + rsr[k, q - 1].astype(jnp.float32)
        if k == 0:
            arr[0, s] = total.astype(jnp.bfloat16)
            z_spread[0] = spread(zs_send, zs_recv, 0, arr.at[0, s])
            return
        gsum[k - 1] = total.astype(jnp.bfloat16)
        z_copies[k] = []
        for h, span in halves(k):
            copy = pltpu.make_async_remote_copy(
                src_ref=gsum.at[k - 1, span],
                dst_ref=arr.at[k, s, span],
                send_sem=z_send.at[k, h],
                recv_sem=z_recv.at[k, h],
                device_id={"grp": partners(me, k, G)[1]},
                device_id_type=MESH,
            )
            copy.start()
            sends.append(copy)
            z_copies[k].append(copy)

    load_x[0].wait()
    load_c.wait()
    project(0)
    gradients(0)
    group_sum(0)

    for n, ks in enumerate(plan):
        if n == 0:
            fetch[ks[0]].wait_send()
            for k in late:
                fetch[k].start()
            sends.extend(fetch[k] for k in order[1:] if k != ks[0])
        for k in ks:
            take_fetch(k)
        for k in ks:
            project(k)
        for k in ks:
            gradients(k)
        for k in ks:
            group_sum(k)

    outs = []

    def put_out(k):
        for copy in z_spread[k]:
            copy.wait_recv()
        copy = pltpu.make_async_copy(arr.at[k], out_ref.at[k], out_sem.at[k])
        copy.start()
        outs.append(copy)

    put_out(0)
    for j in range(T):
        if j:
            load_x[j].wait()
        load_w[j].wait()
        term = jnp.dot(xv[j], wv[j], preferred_element_type=jnp.float32)
        acc[...] = term if j == 0 else acc[...] + term
    low_all = wide[...].reshape(G * full, rows)
    b_all = fetched[:, :, :, pl.ds(wa, wb)].reshape(G * full, wb)
    delta = lax.dot_general(
        low_all, b_all, (((0,), (0,)), ((), ())), preferred_element_type=jnp.float32
    )
    proj_ref[...] = (acc[...] + SCALE * delta).astype(jnp.bfloat16)

    for k in order[1:]:
        z_spread[k] = []
        for h, span in halves(k):
            z_copies[k][h].wait_recv()
            z_spread[k] += spread(zs_send, zs_recv, k, arr.at[k, s, span], h)
        if k not in late:
            put_out(k)
    for k in late:
        put_out(k)
    for copy in outs:
        copy.wait()
    for copy in sends:
        copy.wait_send()


def owner_kernel(
    dims,
    lists_hbm,
    arr_hbm,
    proj_in,
    proj_ref,
    ga_ref,
    gb_ref,
    lists_ref,
    arr_ref,
    buf_a,
    buf_b,
    proj_v,
    sem,
    load_sem,
):
    G, T, S, share, rank, owned, wa, wb, rows = dims
    me = lax.axis_index("grp")
    slots = S * share
    load_l = pltpu.make_async_copy(lists_hbm, lists_ref, load_sem.at[0])
    load_l.start()
    load_arr = pltpu.make_async_copy(arr_hbm, arr_ref, load_sem.at[1])
    load_arr.start()
    load_p = pltpu.make_async_copy(proj_in, proj_v, load_sem.at[2])
    load_p.start()
    buf_a[...] = jnp.zeros_like(buf_a)
    buf_b[...] = jnp.zeros_like(buf_b)
    load_l.wait()
    targets = []
    for k in range(G):
        group, _ = partners(me, k, G)
        for c in range(slots):
            t = lists_ref[group, me, c]
            targets.append(jnp.where(t >= 0, t - me * owned, owned))
    load_p.wait()
    copies = [pltpu.make_async_copy(proj_v, proj_ref, sem.at[0])]
    copies[0].start()
    load_arr.wait()
    for i, row in enumerate(targets):
        buf_a[row] += arr_ref[i, :, :wa].astype(jnp.float32)
        buf_b[row] += arr_ref[i, :, wa:].astype(jnp.float32)
    for n, (buf, out) in enumerate(((buf_a, ga_ref), (buf_b, gb_ref))):
        copies.append(pltpu.make_async_copy(buf.at[pl.ds(0, owned)], out, sem.at[n + 1]))
        copies[-1].start()
    for copy in copies:
        copy.wait()


def body(tokens, base_weight, adapter_a, adapter_b, token_tenant, tenant_lists, cotangent):
    G = lax.axis_size("grp")
    T = lax.axis_size("tp")
    S = lax.axis_size("seq")
    owned, rank, wa = adapter_a.shape
    wb = adapter_b.shape[2]
    depth = tenant_lists.shape[2]
    rows = tokens.shape[0]
    share = -(-depth // S)
    if share * S != depth:
        tenant_lists = jnp.pad(
            tenant_lists, ((0, 0), (0, 0), (0, share * S - depth)), constant_values=-1
        )
    R = share * rank
    width = wa + wb
    slots = share * S
    dims = (G, T, S, share, rank, owned, wa, wb, rows)
    bf, f32 = jnp.bfloat16, jnp.float32
    vmem = pl.BlockSpec(memory_space=pltpu.VMEM)
    hbm = pl.BlockSpec(memory_space=pl.ANY)
    dma = pltpu.SemaphoreType.DMA
    proj, arrived = pl.pallas_call(
        functools.partial(exchange_kernel, dims),
        out_shape=(
            jax.ShapeDtypeStruct((rows, wb), bf),
            jax.ShapeDtypeStruct((G, S, R, width), bf),
        ),
        in_specs=[hbm] * 7,
        out_specs=(vmem, hbm),
        scratch_shapes=[
            pltpu.SMEM((G, G, share * S), jnp.int32),
            pltpu.VMEM((1, rows), jnp.int32),
            pltpu.VMEM((T, rows, wa), bf),
            pltpu.VMEM((T, wa, wb), bf),
            pltpu.VMEM((owned, rank, wa), bf),
            pltpu.VMEM((owned, rank, wb), bf),
            pltpu.VMEM((rows, wb), bf),
            pltpu.VMEM((G, S, R, width), bf),
            pltpu.VMEM((G - 1, R, width), bf),
            pltpu.VMEM((G, 2 * rank, rows), bf),
            pltpu.VMEM((G, T - 1, 2 * rank, rows), bf),
            pltpu.VMEM((G, S * R, rows), bf),
            pltpu.VMEM((G, S, R, width), bf),
            pltpu.VMEM((G, S - 1, R, width), bf),
            pltpu.VMEM((G - 1, R, width), bf),
            pltpu.VMEM((G, S, R, width), bf),
            pltpu.VMEM((rows, wb), f32),
            dma((5 + 2 * T,)),
            dma((G,)),
            dma((G,)),
            dma((G,)),
            dma((G, S, 1)),
            dma((G, S, 1)),
            dma((G, T)),
            dma((G, T)),
            dma((G, S)),
            dma((G, S)),
            dma((G, 2)),
            dma((G, 2)),
            dma((G, S, 2)),
            dma((G, S, 2)),
        ],
        compiler_params=pltpu.CompilerParams(
            collective_id=0, has_side_effects=True, vmem_limit_bytes=64 * 2**20
        ),
        name="exchange",
    )(
        tenant_lists,
        token_tenant.reshape(1, rows),
        tokens,
        base_weight,
        adapter_a,
        adapter_b,
        cotangent,
    )
    return pl.pallas_call(
        functools.partial(owner_kernel, dims),
        out_shape=(
            jax.ShapeDtypeStruct((rows, wb), bf),
            jax.ShapeDtypeStruct((owned, rank, wa), f32),
            jax.ShapeDtypeStruct((owned, rank, wb), f32),
        ),
        in_specs=[hbm, hbm, hbm],
        out_specs=(hbm, hbm, hbm),
        scratch_shapes=[
            pltpu.SMEM((G, G, slots), jnp.int32),
            pltpu.VMEM((G * slots, rank, width), bf),
            pltpu.VMEM((owned + 1, rank, wa), f32),
            pltpu.VMEM((owned + 1, rank, wb), f32),
            pltpu.VMEM((rows, wb), bf),
            dma((3,)),
            dma((3,)),
        ],
        compiler_params=pltpu.CompilerParams(vmem_limit_bytes=64 * 2**20),
        name="owner_sums",
    )(tenant_lists, arrived.reshape(G * S * share, rank, width), proj)


def solution(mesh):
    return jax.shard_map(
        body,
        mesh=mesh,
        in_specs=(
            P(("grp", "seq"), None),
            P(None, "tp"),
            P("grp", None, "tp"),
            P("grp", None, "tp"),
            P(("grp", "seq")),
            P(),
            P(("grp", "seq"), "tp"),
        ),
        out_specs=(P(("grp", "seq"), "tp"), P("grp", None, "tp"), P("grp", None, "tp")),
        check_vma=False,
    )
```
